256 devices in a mesh: dp: 32 (over z, y_hi, core), tensor: 8 (over x, y_lo).
Axes of the slice: x: 4, y: 4 (y_hi: 2, y_lo: 2; y = y_hi * 2 + y_lo), z: 8, core: 2. Of those that a mesh axis runs over, the one named last changes fastest.
Arguments:
- activations: bfloat16 [16384, 18432], P('dp', 'tensor'), may hold values from -28 to 28
- old_codes: bfloat16 [2304, 8, 1024], P('dp', None, 'tensor'), may hold values from -1 to 1
- old_scales: float32 [2304, 8, 8], P('dp', None, 'tensor'), may hold values from 0.0002 to 0.002
Outputs:
- new_codes: bfloat16 [2304, 8, 1024], P('dp', None, 'tensor')
- new_scales: float32 [2304, 8, 8], P('dp', None, 'tensor')
The draws below stay inside these ranges and needn't reach their ends.
All inputs are finite; a program needn't handle non-finite values. Where the reference program divides by a largest or mean magnitude, that divisor is 1e-20 or more.
Results may differ from the reference program's by a relative error of at most 0.0015.
Values may be sent and summed in bfloat16 or wider, within the bound.
A program may use at most 64 MiB of HBM per device.

```python
import math
import jax
import jax.numpy as jnp
from jax import lax

WIDTH = 18432
TOK_DEV = 512
ROWB = 128
QB = 128
BLOCK = 2304
ROWS = 1024
TOKENS = 16384
N_DP = 32
N_TENSOR = 8


def draw_activations(key, part):
    key = jax.random.fold_in(key, 11)
    key_values, key_tokens, key_features = jax.random.split(key, 3)
    position = jnp.arange(TOKENS, dtype=jnp.float32) / TOKENS
    token_scale = jnp.exp(jnp.log(3.0) * (position - 0.5)) * jnp.exp(jax.random.uniform(key_tokens, (TOKENS,), jnp.float32, -0.2, 0.2))
    values = jax.random.truncated_normal(key_values, -4.0, 4.0, (TOKENS, WIDTH), jnp.float32)
    feature_scale = jnp.exp(jax.random.uniform(key_features, (WIDTH,), jnp.float32, jnp.log(0.3), jnp.log(3.0)))
    return (values * token_scale[:, None] * feature_scale[None, :]).astype(jnp.bfloat16)


def level_of(key, extent, pieces, smallest, top_value):
    def one(dim, blocks):
        steps = jax.random.uniform(jax.random.fold_in(jax.random.fold_in(key, 6), dim), (blocks,), jnp.float32, smallest / len(pieces), top_value / len(pieces))
        return jnp.repeat(jnp.exp(steps), extent[dim] // blocks).reshape((-1,) + (1,) * (len(extent) - dim - 1))

    factor_of = one(*pieces[0])
    for cut in pieces[1:]:
        factor_of = factor_of * one(*cut)
    return factor_of


def setup_inputs(seed: int = 0) -> dict:
    seeds = jax.random.split(jax.random.key(seed), 4)
    activations = draw_activations(jax.random.fold_in(seeds[3], 71), 0)
    old_codes = jnp.clip(jax.random.uniform(seeds[1], (BLOCK, N_TENSOR, ROWS), jnp.float32, -1.0, 1.0) * level_of(seeds[1], (BLOCK, N_TENSOR, ROWS), ((0, 32), (2, 8)), -0.4, 0.0), -1.0, 1.0).astype(jnp.bfloat16)
    old_scales = jnp.clip(jnp.exp(math.log(0.002) - 2.3025852 * jax.random.uniform(seeds[2], (BLOCK, N_TENSOR, ROWS // QB), jnp.float32) ** level_of(seeds[2], (BLOCK, N_TENSOR, ROWS // QB), ((0, 32), (2, 8)), -0.2, 0.2)), 0.0002, 0.002)
    return dict(activations=activations, old_codes=old_codes, old_scales=old_scales)


decay_rate = 0.95


def shard_products(span):
    window = span.reshape(TOK_DEV, N_TENSOR, BLOCK)[:, :, :ROWB].reshape(TOK_DEV, ROWS)
    return lax.dot_general(span, window, (((0,), (0,)), ((), ())), preferred_element_type=jnp.float32)


def reference(activations, old_codes, old_scales):
    shards = activations.reshape(N_DP, TOK_DEV, WIDTH)

    def accumulate(total, span):
        return total + shard_products(span), None

    products, unused = lax.scan(accumulate, jnp.zeros((WIDTH, ROWS), jnp.float32), shards)
    products = jnp.transpose(products.reshape(N_TENSOR, BLOCK, ROWS), (1, 0, 2))
    expand = jnp.repeat(old_scales, QB, axis=2)
    statistic = decay_rate * old_codes.astype(jnp.float32) * expand + (1.0 - decay_rate) * products / TOKENS
    blocks = statistic.reshape(BLOCK, N_TENSOR, ROWS // QB, QB)
    new_scales = jnp.max(jnp.abs(blocks), axis=3) + 1e-6
    new_codes = (blocks / new_scales[..., None]).reshape(BLOCK, N_TENSOR, ROWS).astype(jnp.bfloat16)
    return new_codes, new_scales
```

```python
import jax
import jax.numpy as jnp
from jax import lax
from jax.sharding import PartitionSpec as P

ROWB = 128
QB = 128


decay_rate = 0.95
contract = (((0,), (0,)), ((), ()))


def local(activations, old_codes, old_scales):
    tensor_count = lax.axis_size("tensor")
    tokens_all = activations.shape[0] * lax.axis_size("dp")
    windows = lax.all_gather(activations[:, :ROWB], "tensor", axis=1, tiled=True)
    partial_value = lax.dot_general(
        activations, windows, contract, preferred_element_type=jnp.float32
    )
    summed = lax.psum_scatter(partial_value, "dp", scatter_dimension=0, tiled=True)
    products = lax.all_to_all(
        summed.reshape(summed.shape[0], tensor_count, ROWB), "tensor", 1, 1, tiled=False
    )
    expand = jnp.repeat(old_scales, QB, axis=2)
    statistic = (
        decay_rate * old_codes.astype(jnp.float32) * expand
        + (1.0 - decay_rate) * products / tokens_all
    )
    blocks = statistic.reshape(statistic.shape[0], statistic.shape[1], ROWB // QB, QB)
    new_scales = jnp.max(jnp.abs(blocks), axis=3) + 1e-06
    new_codes = (blocks / new_scales[..., None]).reshape(statistic.shape).astype(jnp.bfloat16)
    return (new_codes, new_scales)


def solution(mesh):
    placed = (P("dp", "tensor"), P("dp", None, "tensor"), P("dp", None, "tensor"))
    return jax.shard_map(
        local,
        mesh=mesh,
        in_specs=placed,
        out_specs=(P("dp", None, "tensor"), P("dp", None, "tensor")),
        check_vma=False,
    )
```

```python
import functools

import jax
import jax.numpy as jnp
from jax import lax
from jax.experimental import pallas as pl
from jax.experimental.pallas import tpu as pltpu
from jax.sharding import PartitionSpec as P

ROWB = 128
QB = 128
NX, NZ = 4, 8
SLAB = 144
HALF = 72
CODED = False

decay_rate = 0.95
MESH = pl.DeviceIdType.MESH

SHIFT = (0, 1, 3, 2)
CHAINS = (
    (0, False, True, 1),
    (0, False, False, 1),
    (1, True, False, -1),
    (2, True, False, 1),
    (3, False, True, -1),
    (3, False, False, -1),
)
TIMES = (
    (0.0, 4.0, 8.0, 12.0, 16.0),
    (0.1, 4.1, 8.1, 12.1, 16.1),
    (6.0, 9.5, 13.0, 16.5, 20.0),
    (15.0, 18.5, 22.0, 25.5, 29.0),
    (10.0, 14.0, 18.0, 22.0, 26.0),
    (10.1, 14.1, 18.1, 22.1, 26.1),
)
BUILD = (-1.0, 2.0, 5.0, 9.9)


def enc(v):
    return v


def dec(v):
    return v


def kernel(act, out, a_v, wown, at2, wbuf, p, zsend, zrecv, ysend, yrecv, rsend, rrecv, fbuf, frecv,
           hs_sem, a_ss, a_rs, w_ss, w_rs, v_ss, v_rs, z_ss, z_rs, y_ss, y_rs, r_ss, r_rs, f_ss, f_rs):
    d, t = lax.axis_index("dp"), lax.axis_index("tensor")
    x, l = t // 2, lax.rem(t, 2)
    z, h, c = d // 4, lax.rem(d // 2, 2), lax.rem(d, 2)

    def dev(dx=0, dz=0, hh=h, ll=l, cc=c):
        return {
            "dp": (lax.rem(z + dz + NZ, NZ) * 2 + hh) * 2 + cc,
            "tensor": lax.rem(x + dx, NX) * 2 + ll,
        }

    def remote(src, dst, ss, rs, to):
        return pltpu.make_async_remote_copy(
            src_ref=src, dst_ref=dst, send_sem=ss, recv_sem=rs, device_id=to, device_id_type=MESH
        )

    n_ch = a_ss.shape[0]
    width = a_v.shape[1]
    cw = width // n_ch
    load_w = pltpu.make_async_copy(act.at[:, pl.ds(0, ROWB)], wown, hs_sem.at[n_ch])
    load_w.start()
    loads = [
        pltpu.make_async_copy(
            act.at[:, pl.ds(i * cw, cw)], a_v.at[:, pl.ds(i * cw, cw)], hs_sem.at[i]
        )
        for i in range(n_ch)
    ]
    for cp in loads:
        cp.start()

    barrier = pltpu.get_barrier_semaphore()
    peers = [dev(dx, 0, h, lax.rem(l + dl, 2), lax.rem(c + dc, 2))
             for dx in range(NX) for dl in range(2) for dc in range(2) if dx or dl or dc]
    peers += [dev(dz=1), dev(dz=-1), dev(hh=1 - h)]
    for peer in peers:
        pl.semaphore_signal(barrier, inc=1, device_id=peer, device_id_type=MESH)
    pl.semaphore_wait(barrier, len(peers))

    sent = []
    load_w.wait()
    w_y = remote(wown, wbuf.at[0, c], w_ss.at[0], w_rs.at[c], dev(ll=1 - l, cc=l))
    w_y.start()
    sent.append(w_y)
    w_c = remote(wown, wbuf.at[0, c], w_ss.at[1], w_rs.at[c], dev(cc=1 - c))

    @pl.when(c != l)
    def _():
        w_c.start()

    @pl.when(c == l)
    def _():
        wbuf[0, c] = wown[...]

    swaps = []
    for i in range(n_ch):
        loads[i].wait()
        for b in range(cw // 128):
            lo = i * cw + b * 128
            at2[c, pl.ds(lo, 128), :] = a_v[:, lo:lo + 128].T
        part = at2.at[c, pl.ds(i * cw, cw), :]
        cp = remote(part, part, a_ss.at[i], a_rs.at[i], dev(cc=1 - c))
        cp.start()
        swaps.append(cp)
        if i == 0:
            w_in = remote(wown, wbuf.at[0, 1 - c], w_ss.at[0], w_rs.at[1 - c], dev(cc=1 - c))
            w_in.wait_recv()

            @pl.when(c != l)
            def _():
                w_y.wait_recv()

            win = {}
            for j, dx in ((1, 3), (2, 1), (3, 2)):
                win[j] = remote(wbuf.at[0], wbuf.at[j], v_ss.at[j], v_rs.at[j], dev(dx))
                win[j].start()
                sent.append(win[j])
    sent += swaps
    for cp in swaps:
        cp.wait_recv()

    def slab(off, other):
        hh = 1 - h if other else h
        return lax.rem(z + off + 2 * NZ, NZ) * 2 + hh

    def y_copy(q, n, src):
        return remote(src, yrecv.at[q, n], y_ss.at[q, n], y_rs.at[q, n], dev(hh=1 - h))

    def build(j, first, last):
        yfirst, sgn = [(ch[1], ch[3]) for ch in CHAINS if ch[0] == j][0]

        def body(n, carry):
            odd = lax.rem(n, 2)
            off = sgn * jnp.where(odd == 1, n // 2 - 3, 4 - n // 2)
            zs = lax.rem(z + off + 2 * NZ, NZ)
            rows = pl.ds(pl.multiple_of(zs * (2 * SLAB), 2 * SLAB), 2 * SLAB)
            res = jnp.dot(at2[0, rows, :], wbuf[j, 0], preferred_element_type=jnp.float32)
            res += jnp.dot(at2[1, rows, :], wbuf[j, 1], preferred_element_type=jnp.float32)
            p[j, zs * 2] = res[:SLAB]
            p[j, zs * 2 + 1] = res[SLAB:]
            if yfirst:
                q = j - 1
                if CODED:
                    ysend[q, n] = enc(p[j, zs * 2 + 1 - h])
                    y_copy(q, n, ysend.at[q, n]).start()
                else:
                    y_copy(q, n, p.at[j, zs * 2 + 1 - h]).start()
            return carry

        lax.fori_loop(first, last, body, 0)

    def z_copy(u, m, src, to):
        return remote(src, zrecv.at[u, m], z_ss.at[u, m], z_rs.at[u, m], dev(dz=to))

    def taken(u, m):
        j, yfirst, other, sgn = CHAINS[u]
        cp = z_copy(u, m, zsend.at[u, m] if CODED else p.at[j, slab(0, other)], sgn if m < 4 else -sgn)
        cp.wait_recv()
        return dec(zrecv[u, m])

    def own(u, n, off):
        j, yfirst, other, sgn = CHAINS[u]
        v = p[j, slab(off, other)]
        if yfirst:
            cp = y_copy(j - 1, n, ysend.at[j - 1, n] if CODED else p.at[j, slab(off, other)])
            cp.wait_recv()
            v = v + dec(yrecv[j - 1, n])
        return v

    def step(u, k):
        j, yfirst, other, sgn = CHAINS[u]
        todo = [(k, 2 * k, sgn * (4 - k), sgn)]
        if k < 3:
            todo.append((4 + k, 2 * k + 1, -sgn * (3 - k), -sgn))
        for m, n, off, to in todo:
            v = own(u, n, off)
            if k:
                v = v + taken(u, m - 1)
            if CODED:
                zsend[u, m] = enc(v)
                cp = z_copy(u, m, zsend.at[u, m], to)
            else:
                if k or yfirst:
                    p[j, slab(off, other)] = v
                cp = z_copy(u, m, p.at[j, slab(off, other)], to)
            cp.start()
            sent.append(cp)

    def spread(j, v):
        fbuf[j, 0] = v[:HALF]
        fbuf[j, 1] = v[HALF:]
        for cc in range(2):
            cp = remote(fbuf.at[j, cc], frecv.at[t], f_ss.at[j, cc], f_rs.at[t], dev(SHIFT[j], ll=c, cc=cc))
            if j:
                cp.start()
                sent.append(cp)
            else:
                away = jnp.logical_or(l != c, c != cc)

                @pl.when(away)
                def _():
                    cp.start()

                @pl.when(jnp.logical_not(away))
                def _():
                    frecv[t] = fbuf[0, cc]

                late.append((away, cp))

    late = []

    def finish(u):
        j, yfirst, other, sgn = CHAINS[u]
        v = own(u, 7, 0) + taken(u, 3) + taken(u, 6)
        if yfirst:
            spread(j, v)
            return
        q = j // 3
        cp = remote(rsend.at[q], rrecv.at[q], r_ss.at[q], r_rs.at[q], dev(hh=1 - h))
        if other:
            rsend[q] = v
            cp.start()
            sent.append(cp)
        else:
            cp.wait_recv()
            spread(j, v + rrecv[q])

    def arrive(j):
        if j:
            win[j].wait_recv()

    tasks = []
    for u, times in enumerate(TIMES):
        for k in range(4):
            tasks.append((times[k], functools.partial(step, u, k)))
        tasks.append((times[4], functools.partial(finish, u)))
    for j, when in enumerate(BUILD):
        tasks.append((when, functools.partial(arrive, j)))
        if j == 0 or j == 3:
            tasks.append((when + 0.001, functools.partial(build, j, 0, 2)))
            tasks.append((when + 1.5, functools.partial(build, j, 2, 8)))
        else:
            tasks.append((when + 0.001, functools.partial(build, j, 0, 8)))
    tasks.sort(key=lambda item: item[0])
    for _, run in tasks:
        run()

    for dx in range(NX):
        for ll in range(2):
            s = lax.rem(x + dx, NX) * 2 + lax.rem(l + ll, 2)
            cp = remote(fbuf.at[0, 0], frecv.at[s], f_ss.at[0, 0], f_rs.at[s], dev(cc=1 - c))
            if dx or ll:
                cp.wait_recv()
            else:
                pl.when(c != l)(cp.wait_recv)
    out[...] = frecv[...]

    for cp in sent:
        cp.wait_send()
    pl.when(c != l)(w_c.wait_send)
    for away, cp in late:
        pl.when(away)(cp.wait_send)
    for q in range(2):
        for n in range(8):
            y_copy(q, n, ysend.at[q, n] if CODED else p.at[q + 1, n]).wait_send()


def products_of(activations):
    tokens, width = activations.shape
    link = jnp.bfloat16 if CODED else jnp.float32
    dma = pltpu.SemaphoreType.DMA
    n_ch = 3
    small = (SLAB, ROWB)
    return pl.pallas_call(
        kernel,
        out_shape=jax.ShapeDtypeStruct((8, HALF, ROWB), jnp.float32),
        in_specs=[pl.BlockSpec(memory_space=pl.ANY)],
        out_specs=pl.BlockSpec(memory_space=pltpu.VMEM),
        scratch_shapes=[
            pltpu.VMEM((tokens, width), jnp.bfloat16),
            pltpu.VMEM((tokens, ROWB), jnp.bfloat16),
            pltpu.VMEM((2, width, tokens), jnp.bfloat16),
            pltpu.VMEM((4, 2, tokens, ROWB), jnp.bfloat16),
            pltpu.VMEM((4, 2 * NZ) + small, jnp.float32),
            pltpu.VMEM((6, 7) + small if CODED else (1, 1, 16, 128), link),
            pltpu.VMEM((6, 7) + small, link),
            pltpu.VMEM((2, 8) + small if CODED else (1, 1, 16, 128), link),
            pltpu.VMEM((2, 8) + small, link),
            pltpu.VMEM((2,) + small, jnp.float32),
            pltpu.VMEM((2,) + small, jnp.float32),
            pltpu.VMEM((4, 2, HALF, ROWB), jnp.float32),
            pltpu.VMEM((8, HALF, ROWB), jnp.float32),
            dma((n_ch + 1,)),
            dma((n_ch,)), dma((n_ch,)),
            dma((2,)), dma((2,)),
            dma((4,)), dma((4,)),
            dma((6, 7)), dma((6, 7)),
            dma((2, 8)), dma((2, 8)),
            dma((2,)), dma((2,)),
            dma((4, 2)), dma((8,)),
        ],
        compiler_params=pltpu.CompilerParams(
            collective_id=0, has_side_effects=True, vmem_limit_bytes=48 << 20
        ),
        name="summed_products",
    )(activations)


def local(activations, old_codes, old_scales):
    tokens_all = activations.shape[0] * lax.axis_size("dp")
    products = jnp.transpose(products_of(activations), (1, 0, 2))
    statistic = (
        decay_rate * old_codes.astype(jnp.float32) * old_scales
        + (1.0 - decay_rate) * products / tokens_all
    )
    new_scales = jnp.max(jnp.abs(statistic), axis=2, keepdims=True) + 1e-06
    new_codes = (statistic / new_scales).astype(jnp.bfloat16)
    return (new_codes, new_scales)


def solution(mesh):
    placed = (P("dp", "tensor"), P("dp", None, "tensor"), P("dp", None, "tensor"))
    return jax.shard_map(
        local,
        mesh=mesh,
        in_specs=placed,
        out_specs=(P("dp", None, "tensor"), P("dp", None, "tensor")),
        check_vma=False,
    )
```

```python
import functools
import math

import jax
import jax.numpy as jnp
from jax import lax
from jax.experimental import pallas as pl
from jax.experimental.pallas import tpu as pltpu
from jax.sharding import PartitionSpec as P

ROWB = 128
QB = 128
NX, NZ = 4, 8
SLAB = 144
HALF = 72
CODED = True

decay_rate = 0.95
MESH = pl.DeviceIdType.MESH

SHIFT = (0, 1, 3, 2)
CHAINS = (
    (0, False, True, 1),
    (0, False, False, 1),
    (1, True, False, -1),
    (2, True, False, 1),
    (3, False, True, -1),
    (3, False, False, -1),
)
TIMES = (
    (0.0, 4.0, 8.0, 12.0, 16.0),
    (0.1, 4.1, 8.1, 12.1, 16.1),
    (6.0, 9.5, 13.0, 16.5, 20.0),
    (15.0, 18.5, 22.0, 25.5, 29.0),
    (10.0, 14.0, 18.0, 22.0, 26.0),
    (10.1, 14.1, 18.1, 22.1, 26.1),
)
BUILD = (-1.0, 2.0, 5.0, 9.9)


LEAST = 2.0 ** -5
UNIT = 2.0 ** -9
FLOOR = LEAST * (LEAST * UNIT) ** 7


def enc(v):
    if not CODED:
        return v
    a = jnp.maximum(jnp.abs(v), LEAST) * UNIT
    a2 = a * a
    return (v * ((a2 * a2) * (a2 * a))).astype(jnp.bfloat16)


def dec(y):
    if not CODED:
        return y
    y = y.astype(jnp.float32)
    a = jnp.log(jnp.maximum(jnp.abs(y), FLOOR))
    return y * jnp.exp(a * -0.875 + 0.875 * math.log(1.0 / UNIT))


def kernel(act, out, a_v, wown, at2, wbuf, p, zsend, zrecv, ysend, yrecv, rsend, rrecv, fbuf, frecv,
           hs_sem, a_ss, a_rs, w_ss, w_rs, v_ss, v_rs, z_ss, z_rs, y_ss, y_rs, r_ss, r_rs, f_ss, f_rs):
    d, t = lax.axis_index("dp"), lax.axis_index("tensor")
    x, l = t // 2, lax.rem(t, 2)
    z, h, c = d // 4, lax.rem(d // 2, 2), lax.rem(d, 2)

    def dev(dx=0, dz=0, hh=h, ll=l, cc=c):
        return {
            "dp": (lax.rem(z + dz + NZ, NZ) * 2 + hh) * 2 + cc,
            "tensor": lax.rem(x + dx, NX) * 2 + ll,
        }

    def remote(src, dst, ss, rs, to):
        return pltpu.make_async_remote_copy(
            src_ref=src, dst_ref=dst, send_sem=ss, recv_sem=rs, device_id=to, device_id_type=MESH
        )

    n_ch = a_ss.shape[0]
    width = a_v.shape[1]
    cw = width // n_ch
    load_w = pltpu.make_async_copy(act.at[:, pl.ds(0, ROWB)], wown, hs_sem.at[n_ch])
    load_w.start()
    loads = [
        pltpu.make_async_copy(
            act.at[:, pl.ds(i * cw, cw)], a_v.at[:, pl.ds(i * cw, cw)], hs_sem.at[i]
        )
        for i in range(n_ch)
    ]
    for cp in loads:
        cp.start()

    barrier = pltpu.get_barrier_semaphore()
    peers = [dev(dx, 0, h, lax.rem(l + dl, 2), lax.rem(c + dc, 2))
             for dx in range(NX) for dl in range(2) for dc in range(2) if dx or dl or dc]
    peers += [dev(dz=1), dev(dz=-1), dev(hh=1 - h)]
    for peer in peers:
        pl.semaphore_signal(barrier, inc=1, device_id=peer, device_id_type=MESH)
    pl.semaphore_wait(barrier, len(peers))

    sent = []
    load_w.wait()
    w_y = remote(wown, wbuf.at[0, c], w_ss.at[0], w_rs.at[c], dev(ll=1 - l, cc=l))
    w_y.start()
    sent.append(w_y)
    w_c = remote(wown, wbuf.at[0, c], w_ss.at[1], w_rs.at[c], dev(cc=1 - c))

    @pl.when(c != l)
    def _():
        w_c.start()

    @pl.when(c == l)
    def _():
        wbuf[0, c] = wown[...]

    swaps = []
    for i in range(n_ch):
        loads[i].wait()
        for b in range(cw // 128):
            lo = i * cw + b * 128
            at2[c, pl.ds(lo, 128), :] = a_v[:, lo:lo + 128].T
        part = at2.at[c, pl.ds(i * cw, cw), :]
        cp = remote(part, part, a_ss.at[i], a_rs.at[i], dev(cc=1 - c))
        cp.start()
        swaps.append(cp)
        if i == 0:
            w_in = remote(wown, wbuf.at[0, 1 - c], w_ss.at[0], w_rs.at[1 - c], dev(cc=1 - c))
            w_in.wait_recv()

            @pl.when(c != l)
            def _():
                w_y.wait_recv()

            win = {}
            for j, dx in ((1, 3), (2, 1), (3, 2)):
                win[j] = remote(wbuf.at[0], wbuf.at[j], v_ss.at[j], v_rs.at[j], dev(dx))
                win[j].start()
                sent.append(win[j])
    sent += swaps
    for cp in swaps:
        cp.wait_recv()

    def slab(off, other):
        hh = 1 - h if other else h
        return lax.rem(z + off + 2 * NZ, NZ) * 2 + hh

    def y_copy(q, n, src):
        return remote(src, yrecv.at[q, n], y_ss.at[q, n], y_rs.at[q, n], dev(hh=1 - h))

    def build(j, first, last):
        yfirst, sgn = [(ch[1], ch[3]) for ch in CHAINS if ch[0] == j][0]

        def body(n, carry):
            odd = lax.rem(n, 2)
            off = sgn * jnp.where(odd == 1, n // 2 - 3, 4 - n // 2)
            zs = lax.rem(z + off + 2 * NZ, NZ)
            rows = pl.ds(pl.multiple_of(zs * (2 * SLAB), 2 * SLAB), 2 * SLAB)
            res = jnp.dot(at2[0, rows, :], wbuf[j, 0], preferred_element_type=jnp.float32)
            res += jnp.dot(at2[1, rows, :], wbuf[j, 1], preferred_element_type=jnp.float32)
            p[j, zs * 2] = res[:SLAB]
            p[j, zs * 2 + 1] = res[SLAB:]
            if yfirst:
                q = j - 1
                if CODED:
                    ysend[q, n] = enc(p[j, zs * 2 + 1 - h])
                    y_copy(q, n, ysend.at[q, n]).start()
                else:
                    y_copy(q, n, p.at[j, zs * 2 + 1 - h]).start()
            return carry

        lax.fori_loop(first, last, body, 0)

    def z_copy(u, m, src, to):
        return remote(src, zrecv.at[u, m], z_ss.at[u, m], z_rs.at[u, m], dev(dz=to))

    def taken(u, m):
        j, yfirst, other, sgn = CHAINS[u]
        cp = z_copy(u, m, zsend.at[u, m] if CODED else p.at[j, slab(0, other)], sgn if m < 4 else -sgn)
        cp.wait_recv()
        return dec(zrecv[u, m])

    def own(u, n, off):
        j, yfirst, other, sgn = CHAINS[u]
        v = p[j, slab(off, other)]
        if yfirst:
            cp = y_copy(j - 1, n, ysend.at[j - 1, n] if CODED else p.at[j, slab(off, other)])
            cp.wait_recv()
            v = v + dec(yrecv[j - 1, n])
        return v

    def step(u, k):
        j, yfirst, other, sgn = CHAINS[u]
        todo = [(k, 2 * k, sgn * (4 - k), sgn)]
        if k < 3:
            todo.append((4 + k, 2 * k + 1, -sgn * (3 - k), -sgn))
        for m, n, off, to in todo:
            v = own(u, n, off)
            if k:
                v = v + taken(u, m - 1)
            if CODED:
                zsend[u, m] = enc(v)
                cp = z_copy(u, m, zsend.at[u, m], to)
            else:
                if k or yfirst:
                    p[j, slab(off, other)] = v
                cp = z_copy(u, m, p.at[j, slab(off, other)], to)
            cp.start()
            sent.append(cp)

    def spread(j, v):
        fbuf[j, 0] = v[:HALF]
        fbuf[j, 1] = v[HALF:]
        for cc in range(2):
            cp = remote(fbuf.at[j, cc], frecv.at[t], f_ss.at[j, cc], f_rs.at[t], dev(SHIFT[j], ll=c, cc=cc))
            if j:
                cp.start()
                sent.append(cp)
            else:
                away = jnp.logical_or(l != c, c != cc)

                @pl.when(away)
                def _():
                    cp.start()

                @pl.when(jnp.logical_not(away))
                def _():
                    frecv[t] = fbuf[0, cc]

                late.append((away, cp))

    late = []

    def finish(u):
        j, yfirst, other, sgn = CHAINS[u]
        v = own(u, 7, 0) + taken(u, 3) + taken(u, 6)
        if yfirst:
            spread(j, v)
            return
        q = j // 3
        cp = remote(rsend.at[q], rrecv.at[q], r_ss.at[q], r_rs.at[q], dev(hh=1 - h))
        if other:
            rsend[q] = v
            cp.start()
            sent.append(cp)
        else:
            cp.wait_recv()
            spread(j, v + rrecv[q])

    def arrive(j):
        if j:
            win[j].wait_recv()

    tasks = []
    for u, times in enumerate(TIMES):
        for k in range(4):
            tasks.append((times[k], functools.partial(step, u, k)))
        tasks.append((times[4], functools.partial(finish, u)))
    for j, when in enumerate(BUILD):
        tasks.append((when, functools.partial(arrive, j)))
        if j == 0 or j == 3:
            tasks.append((when + 0.001, functools.partial(build, j, 0, 2)))
            tasks.append((when + 1.5, functools.partial(build, j, 2, 8)))
        else:
            tasks.append((when + 0.001, functools.partial(build, j, 0, 8)))
    tasks.sort(key=lambda item: item[0])
    for _, run in tasks:
        run()

    for dx in range(NX):
        for ll in range(2):
            s = lax.rem(x + dx, NX) * 2 + lax.rem(l + ll, 2)
            cp = remote(fbuf.at[0, 0], frecv.at[s], f_ss.at[0, 0], f_rs.at[s], dev(cc=1 - c))
            if dx or ll:
                cp.wait_recv()
            else:
                pl.when(c != l)(cp.wait_recv)
    out[...] = frecv[...]

    for cp in sent:
        cp.wait_send()
    pl.when(c != l)(w_c.wait_send)
    for away, cp in late:
        pl.when(away)(cp.wait_send)
    for q in range(2):
        for n in range(8):
            y_copy(q, n, ysend.at[q, n] if CODED else p.at[q + 1, n]).wait_send()


def products_of(activations):
    tokens, width = activations.shape
    link = jnp.bfloat16 if CODED else jnp.float32
    dma = pltpu.SemaphoreType.DMA
    n_ch = 3
    small = (SLAB, ROWB)
    return pl.pallas_call(
        kernel,
        out_shape=jax.ShapeDtypeStruct((8, HALF, ROWB), jnp.float32),
        in_specs=[pl.BlockSpec(memory_space=pl.ANY)],
        out_specs=pl.BlockSpec(memory_space=pltpu.VMEM),
        scratch_shapes=[
            pltpu.VMEM((tokens, width), jnp.bfloat16),
            pltpu.VMEM((tokens, ROWB), jnp.bfloat16),
            pltpu.VMEM((2, width, tokens), jnp.bfloat16),
            pltpu.VMEM((4, 2, tokens, ROWB), jnp.bfloat16),
            pltpu.VMEM((4, 2 * NZ) + small, jnp.float32),
            pltpu.VMEM((6, 7) + small if CODED else (1, 1, 16, 128), link),
            pltpu.VMEM((6, 7) + small, link),
            pltpu.VMEM((2, 8) + small if CODED else (1, 1, 16, 128), link),
            pltpu.VMEM((2, 8) + small, link),
            pltpu.VMEM((2,) + small, jnp.float32),
            pltpu.VMEM((2,) + small, jnp.float32),
            pltpu.VMEM((4, 2, HALF, ROWB), jnp.float32),
            pltpu.VMEM((8, HALF, ROWB), jnp.float32),
            dma((n_ch + 1,)),
            dma((n_ch,)), dma((n_ch,)),
            dma((2,)), dma((2,)),
            dma((4,)), dma((4,)),
            dma((6, 7)), dma((6, 7)),
            dma((2, 8)), dma((2, 8)),
            dma((2,)), dma((2,)),
            dma((4, 2)), dma((8,)),
        ],
        compiler_params=pltpu.CompilerParams(
            collective_id=0, has_side_effects=True, vmem_limit_bytes=48 << 20
        ),
        name="summed_products",
    )(activations)


def local(activations, old_codes, old_scales):
    tokens_all = activations.shape[0] * lax.axis_size("dp")
    products = jnp.transpose(products_of(activations), (1, 0, 2))
    statistic = (
        decay_rate * old_codes.astype(jnp.float32) * old_scales
        + (1.0 - decay_rate) * products / tokens_all
    )
    new_scales = jnp.max(jnp.abs(statistic), axis=2, keepdims=True) + 1e-06
    new_codes = (statistic / new_scales).astype(jnp.bfloat16)
    return (new_codes, new_scales)


def solution(mesh):
    placed = (P("dp", "tensor"), P("dp", None, "tensor"), P("dp", None, "tensor"))
    return jax.shard_map(
        local,
        mesh=mesh,
        in_specs=placed,
        out_specs=(P("dp", None, "tensor"), P("dp", None, "tensor")),
        check_vma=False,
    )
```

```python
import math

import jax
import jax.numpy as jnp
from jax import lax
from jax.experimental import pallas as pl
from jax.experimental.pallas import tpu as pltpu
from jax.sharding import PartitionSpec as P

ROWB = 128
QB = 128
NX, NZ = 4, 8
SLAB = 144
HALF = 72

decay_rate = 0.95
MESH = pl.DeviceIdType.MESH

OWNERS = (((0, 0), (1, 0), (2, 0), (3, 1)), ((3, 0), (0, 1), (1, 1), (2, 1)))
PLACE = {where: (core, j) for core in range(2) for j, where in enumerate(OWNERS[core])}
RING = ((4, 1), (-3, -1), (3, 1), (-2, -1), (2, 1), (-1, -1), (1, 1))
THREE = ((4, 1), (-3, -1), (2, 1), (3, 2), (-2, -1), (-1, -1), (1, 1))
TWO = ((4, 1), (2, 1), (-3, -1), (3, 3), (1, 1), (-2, -2), (-1, -1))
CHAINS = (
    (0, False, True, 1, THREE),
    (0, False, False, 1, THREE),
    (1, False, True, -1, RING),
    (1, False, False, -1, RING),
    (2, True, False, -1, THREE),
    (3, True, False, 1, TWO),
)
YFIRST = [j for j in range(4) if any(ch[0] == j and ch[1] for ch in CHAINS)]
HOPS = sorted({abs(hop) for ch in CHAINS for _, hop in ch[4]})
ORDER = (
    (0, 0, 0), (2, 0, 0), (3, 0, 0), (3, 1, 0), (3, 0, 1), (1, 0, 0), (2, 1, 0), (2, 0, 1), (3, 1, 1), (3, 2, 0),
    (3, 3, 0), (2, 1, 1), (3, 2, 1), (5, 0, 0), (2, 2, 0), (3, 3, 1), (2, 2, 1), (3, 0, 3), (3, 2, 2), (3, 0, 2),
    (3, 1, 3), (2, 3, 0), (3, 0, 4), (3, 1, 2), (2, 3, 1), (3, 3, 2), (3, 4, 0), (3, 4, 1), (3, 1, 4), (3, 2, 3),
    (3, 2, 4), (3, 3, 3), (3, 4, 2), (3, 3, 4), (3, 0, 5), (3, 4, 3), (3, 0, 6), (3, 1, 5), (3, 4, 4), (3, 1, 6),
    (3, 5, 0), (3, 2, 6), (3, 5, 1), (3, 2, 5), (3, 5, 2), (3, 3, 5), (3, 3, 6), (3, 4, 6), (4, 0, 0), (3, 5, 6),
    (3, 4, 5), (3, 5, 3), (3, 5, 4), (3, 5, 5), (4, 1, 0), (4, 2, 0), (4, 3, 0), (4, 4, 0), (4, 5, 0),
)

LEAST = 2.0 ** -5
UNIT = 2.0 ** -9
FLOOR = LEAST * (LEAST * UNIT) ** 7


def enc(v):
    a = jnp.maximum(jnp.abs(v), LEAST) * UNIT
    a2 = a * a
    return (v * ((a2 * a2) * (a2 * a))).astype(jnp.bfloat16)


def dec(y):
    y = y.astype(jnp.float32)
    a = jnp.log(jnp.maximum(jnp.abs(y), FLOOR))
    return y * jnp.exp(a * -0.875 + 0.875 * math.log(1.0 / UNIT))


def kernel(act, out, a_v, wown, wnext, at2, wbuf, p, zsend, zrecv, ysend, yrecv, fbuf, frecv,
           l_sem, a_ss, a_rs, w_ss, w_rs, n_ss, n_rs, z_ss, z_rs, y_ss, y_rs, f_ss, f_rs):
    d, t = lax.axis_index("dp"), lax.axis_index("tensor")
    x, l = t // 2, lax.rem(t, 2)
    z, h, c = d // 4, lax.rem(d // 2, 2), lax.rem(d, 2)

    def dev(dx=0, dz=0, hh=h, ll=l, cc=c):
        return {
            "dp": (lax.rem(z + dz + NZ, NZ) * 2 + hh) * 2 + cc,
            "tensor": lax.rem(x + dx + NX, NX) * 2 + ll,
        }

    def remote(src, dst, ss, rs, to):
        return pltpu.make_async_remote_copy(
            src_ref=src, dst_ref=dst, send_sem=ss, recv_sem=rs, device_id=to, device_id_type=MESH
        )

    def slab(off, other):
        return lax.rem(z + off + 2 * NZ, NZ) * 2 + (1 - h if other else h)

    def owner(j):
        (x0, l0), (x1, l1) = OWNERS[0][j], OWNERS[1][j]
        return x0 + c * (x1 - x0), lax.rem(l + l0 + c * (l1 - l0), 2)

    n_ch = l_sem.shape[0] - 1
    cw = a_v.shape[1] // n_ch
    load_w = pltpu.make_async_copy(act.at[:, pl.ds(0, ROWB)], wown, l_sem.at[n_ch])
    load_w.start()
    loads = []
    for i in range(n_ch):
        part = pl.ds(i * cw, cw)
        loads.append(pltpu.make_async_copy(act.at[:, part], a_v.at[:, part], l_sem.at[i]))
        loads[i].start()
    barrier = pltpu.get_barrier_semaphore()
    greet = [dev(dx, ll=lax.rem(l + dl, 2), cc=lax.rem(c + dc, 2))
             for dx in range(NX) for dl in range(2) for dc in range(2) if dx or dl or dc]
    greet += [dev(dz=s * hop) for hop in HOPS for s in (1, -1)]
    if YFIRST:
        greet.append(dev(hh=1 - h))
    for j, yfirst, other, _, _ in CHAINS:
        if other:
            greet += [dev(-dx, hh=1 - h, ll=lax.rem(l + dl, 2), cc=core)
                      for core in range(2) for dx, dl in (OWNERS[core][j],)]
    for peer in greet:
        pl.semaphore_signal(barrier, inc=1, device_id=peer, device_id_type=MESH)
    for i in range(n_ch):
        loads[i].wait()
        for b in range(cw // 128):
            lo = i * cw + b * 128
            at2[c, pl.ds(lo, 128), :] = a_v[:, lo:lo + 128].T
    load_w.wait()
    pl.semaphore_wait(barrier, len(greet))

    sent = []

    def go(cp):
        cp.start()
        sent.append(cp)

    def share(src, dl, dx):
        core, j = PLACE[dx, dl]
        return remote(src, wbuf.at[j, c], w_ss.at[dl, dx], w_rs.at[j, c], dev(-dx, cc=core))

    def share_here(src, dl):
        core, j = PLACE[0, dl]
        cp = share(src, dl, 0)
        pl.when(c != core)(cp.start)

        @pl.when(c == core)
        def _():
            wbuf[j, core] = src[...]

        late.append((c != core, cp))

    late = []
    w_y = remote(wown, wnext, n_ss, n_rs, dev(ll=1 - l))
    go(w_y)
    go(share(wown, 0, 1))
    go(share(wown, 0, 3))
    share_here(wown, 0)

    swaps = []
    for n in range(NZ):
        zs = lax.rem(z + (n // 2 - 3 if n % 2 else 4 - n // 2) + NZ, NZ)
        part = at2.at[c, pl.ds(pl.multiple_of(zs * (2 * SLAB), 2 * SLAB), 2 * SLAB), :]
        swaps.append(remote(part, part, a_ss.at[n], a_rs.at[n], dev(cc=1 - c)))
        go(swaps[n])
    here = set()

    def need_swaps(upto):
        for n in range(upto):
            if n not in here:
                here.add(n)
                swaps[n].wait_recv()

    def windows(kind):
        if kind == 0:
            go(share(wown, 0, 2))
        elif kind == 1:
            w_y.wait_recv()
            go(share(wnext, 1, 1))
            go(share(wnext, 1, 3))
            share_here(wnext, 1)
        else:
            go(share(wnext, 1, 2))

    def windows_in(j):
        for half in range(2):
            cp = remote(wown, wbuf.at[j, half], w_ss.at[0, 0], w_rs.at[j, half], dev(cc=1 - c))
            own = [core for core in range(2) if OWNERS[core][j][0] == 0 and core == half]
            if own:
                pl.when(c != own[0])(cp.wait_recv)
            else:
                cp.wait_recv()

    def plan_of(j):
        return [ch for ch in CHAINS if ch[0] == j][0]

    def y_copy(q, n):
        return remote(ysend.at[q, n], yrecv.at[q, n], y_ss.at[q, n], y_rs.at[q, n], dev(hh=1 - h))

    def build(j, part):
        _, yfirst, _, sgn, plan = plan_of(j)
        first, last = ((0, 2), (2, 8))[part]
        if part == 0:
            windows_in(j)
        offs = [off * sgn for off, _ in plan] + [0]
        near = {0: 2, 1: 8}[part] if sgn == 1 and plan[:2] == RING[:2] else 8
        need_swaps(near)
        for n in range(first, last):
            zs = lax.rem(z + offs[n] + NZ, NZ)
            rows = pl.ds(pl.multiple_of(zs * (2 * SLAB), 2 * SLAB), 2 * SLAB)
            res = jnp.dot(at2[0, rows, :], wbuf[j, 0], preferred_element_type=jnp.float32)
            res += jnp.dot(at2[1, rows, :], wbuf[j, 1], preferred_element_type=jnp.float32)
            p[j, zs * 2] = res[:SLAB]
            p[j, zs * 2 + 1] = res[SLAB:]
            if yfirst:
                q = YFIRST.index(j)
                ysend[q, n] = enc(p[j, zs * 2 + 1 - h])
                y_copy(q, n).start()

    def z_copy(u, i, hop):
        return remote(zsend.at[u, i], zrecv.at[u, i], z_ss.at[u, i], z_rs.at[u, i], dev(dz=hop))

    def gathered(u, n, off):
        j, yfirst, other, sgn, plan = CHAINS[u]
        v = p[j, slab(off * sgn, other)]
        if yfirst:
            y_copy(YFIRST.index(j), n).wait_recv()
            v = v + dec(yrecv[YFIRST.index(j), n])
        for k, (o, hop) in enumerate(plan):
            if o - hop == off:
                z_copy(u, k, hop * sgn).wait_recv()
                v = v + dec(zrecv[u, k])
        return v

    def pass_on(u, i):
        sgn, plan = CHAINS[u][3:]
        off, hop = plan[i]
        zsend[u, i] = enc(gathered(u, i, off))
        go(z_copy(u, i, hop * sgn))

    def f_copy(u, cc, slot):
        j, _, other, _, _ = CHAINS[u]
        dx, ll = owner(j)
        to = dev(dx, hh=1 - h if other else h, ll=ll, cc=cc)
        return remote(fbuf.at[u, cc], frecv.at[slot, t], f_ss.at[u, cc], f_rs.at[slot, t], to)

    def finish(u, _):
        j, yfirst, other, sgn, plan = CHAINS[u]
        v = gathered(u, 7, 0)
        fbuf[u, 0] = v[:HALF]
        fbuf[u, 1] = v[HALF:]
        for cc in range(2):
            cp = f_copy(u, cc, int(other))
            here_on = [core for core in range(2) if OWNERS[core][j] == (0, 0) and core == cc and not other]
            if not here_on:
                go(cp)
                continue
            pl.when(c != here_on[0])(cp.start)

            @pl.when(c == here_on[0])
            def _():
                frecv[0, t] = fbuf[u, cc]

            late.append((c != here_on[0], cp))

    for kind, one, two in ORDER:
        if kind in (0, 1, 5):
            windows(kind)
        else:
            (build, pass_on, finish)[kind - 2](one, two)

    for (dx, dl), (core, j) in PLACE.items():
        twice = any(ch[0] == j and ch[2] for ch in CHAINS)
        s = lax.rem(x - dx + NX, NX) * 2 + lax.rem(l + dl, 2)
        for slot in range(1 + twice):
            cp = remote(fbuf.at[0, 0], frecv.at[slot, s], f_ss.at[0, 0], f_rs.at[slot, s], dev(cc=1 - c))
            if dx or dl or slot:
                cp.wait_recv()
            else:
                pl.when(c != core)(cp.wait_recv)
        out[s] = frecv[0, s] + frecv[1, s] if twice else frecv[0, s]

    for cp in sent:
        cp.wait_send()
    for away, cp in late:
        pl.when(away)(cp.wait_send)
    for q in range(len(YFIRST)):
        for n in range(8):
            y_copy(q, n).wait_send()


def products_of(activations):
    tokens, width = activations.shape
    dma = pltpu.SemaphoreType.DMA
    n_ch = 3
    small = (SLAB, ROWB)
    n_u, n_y = len(CHAINS), max(len(YFIRST), 1)
    return pl.pallas_call(
        kernel,
        out_shape=jax.ShapeDtypeStruct((8, HALF, ROWB), jnp.float32),
        in_specs=[pl.BlockSpec(memory_space=pltpu.HBM)],
        out_specs=pl.BlockSpec(memory_space=pltpu.VMEM),
        scratch_shapes=[
            pltpu.VMEM((tokens, width), jnp.bfloat16),
            pltpu.VMEM((tokens, ROWB), jnp.bfloat16),
            pltpu.VMEM((tokens, ROWB), jnp.bfloat16),
            pltpu.VMEM((2, width, tokens), jnp.bfloat16),
            pltpu.VMEM((4, 2, tokens, ROWB), jnp.bfloat16),
            pltpu.VMEM((4, 2 * NZ) + small, jnp.float32),
            pltpu.VMEM((n_u, 7) + small, jnp.bfloat16),
            pltpu.VMEM((n_u, 7) + small, jnp.bfloat16),
            pltpu.VMEM((n_y, 8) + small, jnp.bfloat16),
            pltpu.VMEM((n_y, 8) + small, jnp.bfloat16),
            pltpu.VMEM((n_u, 2, HALF, ROWB), jnp.float32),
            pltpu.VMEM((2, 8, HALF, ROWB), jnp.float32),
            dma((n_ch + 1,)),
            dma((NZ,)), dma((NZ,)),
            dma((2, 4)), dma((4, 2)),
            dma, dma,
            dma((n_u, 7)), dma((n_u, 7)),
            dma((n_y, 8)), dma((n_y, 8)),
            dma((n_u, 2)), dma((2, 8)),
        ],
        compiler_params=pltpu.CompilerParams(
            collective_id=0, has_side_effects=True, vmem_limit_bytes=52 << 20
        ),
        name="summed_products",
    )(activations)


def local(activations, old_codes, old_scales):
    tokens_all = activations.shape[0] * lax.axis_size("dp")
    products = jnp.transpose(products_of(activations), (1, 0, 2))
    products, old_codes, old_scales = lax.optimization_barrier((products, old_codes, old_scales))
    statistic = (
        decay_rate * old_codes.astype(jnp.float32) * old_scales
        + (1.0 - decay_rate) * products / tokens_all
    )
    new_scales = jnp.max(jnp.abs(statistic), axis=2, keepdims=True) + 1e-06
    new_codes = (statistic / new_scales).astype(jnp.bfloat16)
    return (new_codes, new_scales)


def solution(mesh):
    placed = (P("dp", "tensor"), P("dp", None, "tensor"), P("dp", None, "tensor"))
    return jax.shard_map(
        local,
        mesh=mesh,
        in_specs=placed,
        out_specs=(P("dp", None, "tensor"), P("dp", None, "tensor")),
        check_vma=False,
    )
```

```python
import math

import jax
import jax.numpy as jnp
from jax import lax
from jax.experimental import pallas as pl
from jax.experimental.pallas import tpu as pltpu
from jax.sharding import PartitionSpec as P

ROWB = 128
QB = 128
NX, NZ = 4, 8
SLAB = 144
HALF = 72
STRIP = 144

decay_rate = 0.95
MESH = pl.DeviceIdType.MESH

OWNERS = (((0, 0), (1, 0), (2, 0), (3, 1)), ((3, 0), (0, 1), (1, 1), (2, 1)))
PLACE = {where: (core, j) for core in range(2) for j, where in enumerate(OWNERS[core])}
RING = ((4, 1), (-3, -1), (3, 1), (-2, -1), (2, 1), (-1, -1), (1, 1))
THREE = ((4, 1), (-3, -1), (2, 1), (3, 2), (-2, -1), (-1, -1), (1, 1))
TWO = ((4, 1), (2, 1), (-3, -1), (3, 3), (1, 1), (-2, -2), (-1, -1))
CHAINS = (
    (0, False, True, 1, THREE),
    (0, False, False, 1, THREE),
    (1, False, True, -1, RING),
    (1, False, False, -1, RING),
    (2, True, False, -1, THREE),
    (3, True, False, 1, TWO),
)
YFIRST = [j for j in range(4) if any(ch[0] == j and ch[1] for ch in CHAINS)]
HOPS = sorted({abs(hop) for ch in CHAINS for _, hop in ch[4]})
ORDER = (
    (0, 0, 0), (1, 0, 0), (2, 0, 0), (3, 0, 0), (3, 0, 1), (3, 1, 0), (2, 1, 0), (3, 1, 1), (3, 3, 1), (3, 2, 0),
    (2, 0, 1), (3, 3, 0), (3, 1, 2), (3, 0, 2), (2, 1, 1), (3, 0, 3), (3, 0, 4), (3, 1, 3), (5, 0, 0), (3, 2, 1),
    (3, 1, 4), (2, 2, 0), (3, 3, 2), (2, 2, 1), (3, 2, 2), (3, 3, 3), (2, 3, 0), (3, 0, 5), (3, 1, 5), (3, 2, 3),
    (3, 0, 6), (3, 4, 0), (3, 3, 4), (3, 4, 1), (2, 3, 1), (3, 2, 4), (3, 4, 2), (3, 1, 6), (3, 2, 5), (3, 4, 3),
    (3, 5, 0), (3, 4, 4), (3, 5, 2), (3, 5, 1), (4, 0, 0), (3, 2, 6), (3, 3, 6), (3, 3, 5), (3, 5, 3), (3, 5, 6),
    (4, 1, 0), (3, 4, 6), (3, 4, 5), (3, 5, 5), (3, 5, 4), (4, 3, 0), (4, 2, 0), (4, 4, 0), (4, 5, 0),
)

LEAST = 2.0 ** -5
UNIT = 2.0 ** -9
FLOOR = LEAST * (LEAST * UNIT) ** 7


def enc(v):
    a = jnp.maximum(jnp.abs(v), LEAST) * UNIT
    a2 = a * a
    return (v * ((a2 * a2) * (a2 * a))).astype(jnp.bfloat16)


def dec(y):
    y = y.astype(jnp.float32)
    a = jnp.log(jnp.maximum(jnp.abs(y), FLOOR))
    return y * jnp.exp(a * -0.875 + 0.875 * math.log(1.0 / UNIT))


def kernel(act, out, a_v, wown, wnext, at2, wbuf, p, zsend, zrecv, ysend, yrecv, fbuf, frecv,
           l_sem, a_ss, a_rs, w_ss, w_rs, n_ss, n_rs, z_ss, z_rs, y_ss, y_rs, f_ss, f_rs):
    d, t = lax.axis_index("dp"), lax.axis_index("tensor")
    x, l = t // 2, lax.rem(t, 2)
    z, h, c = d // 4, lax.rem(d // 2, 2), lax.rem(d, 2)

    def dev(dx=0, dz=0, hh=h, ll=l, cc=c):
        return {
            "dp": (lax.rem(z + dz + NZ, NZ) * 2 + hh) * 2 + cc,
            "tensor": lax.rem(x + dx + NX, NX) * 2 + ll,
        }

    def remote(src, dst, ss, rs, to):
        return pltpu.make_async_remote_copy(
            src_ref=src, dst_ref=dst, send_sem=ss, recv_sem=rs, device_id=to, device_id_type=MESH
        )

    def slab(off, other):
        return lax.rem(z + off + 2 * NZ, NZ) * 2 + (1 - h if other else h)

    def owner(j):
        (x0, l0), (x1, l1) = OWNERS[0][j], OWNERS[1][j]
        return x0 + c * (x1 - x0), lax.rem(l + l0 + c * (l1 - l0), 2)

    n_ch = l_sem.shape[0] - 1
    cw = a_v.shape[1] // n_ch
    load_w = pltpu.make_async_copy(act.at[:, pl.ds(0, ROWB)], wown, l_sem.at[n_ch])
    load_w.start()
    loads = []
    for i in range(n_ch):
        part = pl.ds(i * cw, cw)
        loads.append(pltpu.make_async_copy(act.at[:, part], a_v.at[:, part], l_sem.at[i]))
        loads[i].start()
    barrier = pltpu.get_barrier_semaphore()
    greet = [dev(dx, ll=lax.rem(l + dl, 2), cc=lax.rem(c + dc, 2))
             for dx in range(NX) for dl in range(2) for dc in range(2) if dx or dl or dc]
    greet += [dev(dz=s * hop) for hop in HOPS for s in (1, -1)]
    if YFIRST:
        greet.append(dev(hh=1 - h))
    for j, yfirst, other, _, _ in CHAINS:
        if other:
            greet += [dev(-dx, hh=1 - h, ll=lax.rem(l + dl, 2), cc=core)
                      for core in range(2) for dx, dl in (OWNERS[core][j],)]
    for peer in greet:
        pl.semaphore_signal(barrier, inc=1, device_id=peer, device_id_type=MESH)
    for i in range(n_ch):
        loads[i].wait()

        @pl.loop(0, cw // 128)
        def _(b):
            part = pl.ds(pl.multiple_of(i * cw + b * 128, 128), 128)
            at2[c, part, :] = a_v[:, part].T

    load_w.wait()
    pl.semaphore_wait(barrier, len(greet))

    sent = []

    def go(cp):
        cp.start()
        sent.append(cp)

    def share(src, dl, dx):
        core, j = PLACE[dx, dl]
        return remote(src, wbuf.at[j, c], w_ss.at[dl, dx], w_rs.at[j, c], dev(-dx, cc=core))

    def share_here(src, dl):
        core, j = PLACE[0, dl]
        cp = share(src, dl, 0)
        pl.when(c != core)(cp.start)

        @pl.when(c == core)
        def _():
            wbuf[j, core] = src[...]

        late.append((c != core, cp))

    late = []
    w_y = remote(wown, wnext, n_ss, n_rs, dev(ll=1 - l))
    go(w_y)
    near = [share(wown, 0, 1), share(wown, 0, 3)]
    for cp in near:
        cp.start()
    share_here(wown, 0)

    swaps = []
    for n in range(NZ):
        zs = lax.rem(z + (n // 2 - 3 if n % 2 else 4 - n // 2) + NZ, NZ)
        part = at2.at[c, pl.ds(pl.multiple_of(zs * (2 * SLAB), 2 * SLAB), 2 * SLAB), :]
        swaps.append(remote(part, part, a_ss.at[n], a_rs.at[n], dev(cc=1 - c)))
        go(swaps[n])
    here = set()

    def need_swaps(upto):
        for n in range(upto):
            if n not in here:
                here.add(n)
                swaps[n].wait_recv()

    def windows(kind):
        if kind == 0:
            for cp in near:
                cp.wait_send()
            go(share(wown, 0, 2))
        elif kind == 1:
            w_y.wait_recv()
            go(share(wnext, 1, 1))
            go(share(wnext, 1, 3))
            share_here(wnext, 1)
        else:
            go(share(wnext, 1, 2))

    def windows_in(j):
        for half in range(2):
            cp = remote(wown, wbuf.at[j, half], w_ss.at[0, 0], w_rs.at[j, half], dev(cc=1 - c))
            own = [core for core in range(2) if OWNERS[core][j][0] == 0 and core == half]
            if own:
                pl.when(c != own[0])(cp.wait_recv)
            else:
                cp.wait_recv()

    def plan_of(j):
        return [ch for ch in CHAINS if ch[0] == j][0]

    def y_copy(q, n):
        return remote(ysend.at[q, n], yrecv.at[q, n], y_ss.at[q, n], y_rs.at[q, n], dev(hh=1 - h))

    def build(j, part):
        _, yfirst, _, sgn, plan = plan_of(j)
        first, last = ((0, 2), (2, 8))[part]
        if part == 0:
            windows_in(j)
        offs = [off * sgn for off, _ in plan] + [0]
        near = {0: 2, 1: 8}[part] if sgn == 1 and plan[:2] == RING[:2] else 8
        need_swaps(near)

        @pl.loop(first, last)
        def _(n):
            off = offs[-1]
            for i in range(7):
                off = jnp.where(n == i, offs[i], off)
            zs = lax.rem(z + off + NZ, NZ)
            rows = pl.ds(pl.multiple_of(zs * (2 * SLAB), 2 * SLAB), 2 * SLAB)
            res = jnp.dot(at2[0, rows, :], wbuf[j, 0], preferred_element_type=jnp.float32)
            res += jnp.dot(at2[1, rows, :], wbuf[j, 1], preferred_element_type=jnp.float32)
            p[j, zs * 2] = res[:SLAB]
            p[j, zs * 2 + 1] = res[SLAB:]
            if yfirst:
                q = YFIRST.index(j)

                @pl.loop(0, SLAB, step=STRIP)
                def _(r):
                    rows = pl.ds(pl.multiple_of(r, STRIP), STRIP)
                    ysend[q, n, rows, :] = enc(p[j, zs * 2 + 1 - h, rows, :])

                y_copy(q, n).start()

    def z_copy(u, i, hop):
        return remote(zsend.at[u, i], zrecv.at[u, i], z_ss.at[u, i], z_rs.at[u, i], dev(dz=hop))

    def gathered(u, n, off, put):
        j, yfirst, other, sgn, plan = CHAINS[u]
        terms = []
        if yfirst:
            y_copy(YFIRST.index(j), n).wait_recv()
            terms.append(yrecv.at[YFIRST.index(j), n])
        for k, (o, hop) in enumerate(plan):
            if o - hop == off:
                z_copy(u, k, hop * sgn).wait_recv()
                terms.append(zrecv.at[u, k])
        own = p.at[j, slab(off * sgn, other)]

        @pl.loop(0, SLAB, step=STRIP)
        def _(r):
            rows = pl.ds(pl.multiple_of(r, STRIP), STRIP)
            v = own[rows, :]
            for term in terms:
                v = v + dec(term[rows, :])
            put(rows, v)

    def pass_on(u, i):
        sgn, plan = CHAINS[u][3:]
        off, hop = plan[i]

        def put(rows, v):
            zsend[u, i, rows, :] = enc(v)

        gathered(u, i, off, put)
        go(z_copy(u, i, hop * sgn))

    def f_copy(u, cc, slot):
        j, _, other, _, _ = CHAINS[u]
        dx, ll = owner(j)
        to = dev(dx, hh=1 - h if other else h, ll=ll, cc=cc)
        return remote(fbuf.at[u, pl.ds(cc * HALF, HALF)], frecv.at[slot, t], f_ss.at[u, cc], f_rs.at[slot, t], to)

    def finish(u, _):
        j, yfirst, other, sgn, plan = CHAINS[u]

        def put(rows, v):
            fbuf[u, rows, :] = v

        gathered(u, 7, 0, put)
        for cc in range(2):
            cp = f_copy(u, cc, int(other))
            here_on = [core for core in range(2) if OWNERS[core][j] == (0, 0) and core == cc and not other]
            if not here_on:
                go(cp)
                continue
            pl.when(c != here_on[0])(cp.start)

            @pl.when(c == here_on[0])
            def _():
                frecv[0, t] = fbuf[u, pl.ds(cc * HALF, HALF), :]

            late.append((c != here_on[0], cp))

    for kind, one, two in ORDER:
        if kind in (0, 1, 5):
            windows(kind)
        else:
            (build, pass_on, finish)[kind - 2](one, two)

    for (dx, dl), (core, j) in PLACE.items():
        twice = any(ch[0] == j and ch[2] for ch in CHAINS)
        s = lax.rem(x - dx + NX, NX) * 2 + lax.rem(l + dl, 2)
        for slot in range(1 + twice):
            cp = remote(fbuf.at[0, pl.ds(0, HALF)], frecv.at[slot, s], f_ss.at[0, 0], f_rs.at[slot, s], dev(cc=1 - c))
            if dx or dl or slot:
                cp.wait_recv()
            else:
                pl.when(c != core)(cp.wait_recv)
        out[s] = frecv[0, s] + frecv[1, s] if twice else frecv[0, s]

    for cp in sent:
        cp.wait_send()
    for away, cp in late:
        pl.when(away)(cp.wait_send)
    for q in range(len(YFIRST)):
        for n in range(8):
            y_copy(q, n).wait_send()


def products_of(activations):
    tokens, width = activations.shape
    dma = pltpu.SemaphoreType.DMA
    n_ch = 3
    small = (SLAB, ROWB)
    n_u, n_y = len(CHAINS), max(len(YFIRST), 1)
    return pl.pallas_call(
        kernel,
        out_shape=jax.ShapeDtypeStruct((8, HALF, ROWB), jnp.float32),
        in_specs=[pl.BlockSpec(memory_space=pltpu.HBM)],
        out_specs=pl.BlockSpec(memory_space=pltpu.VMEM),
        scratch_shapes=[
            pltpu.VMEM((tokens, width), jnp.bfloat16),
            pltpu.VMEM((tokens, ROWB), jnp.bfloat16),
            pltpu.VMEM((tokens, ROWB), jnp.bfloat16),
            pltpu.VMEM((2, width, tokens), jnp.bfloat16),
            pltpu.VMEM((4, 2, tokens, ROWB), jnp.bfloat16),
            pltpu.VMEM((4, 2 * NZ) + small, jnp.float32),
            pltpu.VMEM((n_u, 7) + small, jnp.bfloat16),
            pltpu.VMEM((n_u, 7) + small, jnp.bfloat16),
            pltpu.VMEM((n_y, 8) + small, jnp.bfloat16),
            pltpu.VMEM((n_y, 8) + small, jnp.bfloat16),
            pltpu.VMEM((n_u,) + small, jnp.float32),
            pltpu.VMEM((2, 8, HALF, ROWB), jnp.float32),
            dma((n_ch + 1,)),
            dma((NZ,)), dma((NZ,)),
            dma((2, 4)), dma((4, 2)),
            dma, dma,
            dma((n_u, 7)), dma((n_u, 7)),
            dma((n_y, 8)), dma((n_y, 8)),
            dma((n_u, 2)), dma((2, 8)),
        ],
        compiler_params=pltpu.CompilerParams(
            collective_id=0, has_side_effects=True, vmem_limit_bytes=52 << 20
        ),
        name="summed_products",
    )(activations)


def local(activations, old_codes, old_scales):
    tokens_all = activations.shape[0] * lax.axis_size("dp")
    products = jnp.transpose(products_of(activations), (1, 0, 2))
    products, old_codes, old_scales = lax.optimization_barrier((products, old_codes, old_scales))
    statistic = (
        decay_rate * old_codes.astype(jnp.float32) * old_scales
        + (1.0 - decay_rate) * products / tokens_all
    )
    new_scales = jnp.max(jnp.abs(statistic), axis=2, keepdims=True) + 1e-06
    new_codes = (statistic / new_scales).astype(jnp.bfloat16)
    return (new_codes, new_scales)


def solution(mesh):
    placed = (P("dp", "tensor"), P("dp", None, "tensor"), P("dp", None, "tensor"))
    return jax.shard_map(
        local,
        mesh=mesh,
        in_specs=placed,
        out_specs=(P("dp", None, "tensor"), P("dp", None, "tensor")),
        check_vma=False,
    )
```
